128 devices in a mesh: block: 16 (over y, z_hi, core), day: 8 (over z_lo, x).
Axes of the slice: x: 4, y: 4, z: 4 (z_hi: 2, z_lo: 2; z = z_hi * 2 + z_lo), core: 2. Of those that a mesh axis runs over, the one named last changes fastest.
Arguments:
- spectra: bfloat16 [2, 128, 1536, 2048], P(None, None, 'day', 'block'), may hold values from -2000 to 2000
- valid: int32 [1536, 16], P('day', 'block'), may hold values from 0 to 1, as said below
Outputs:
- stacked: float32 [2, 128, 2, 2048, 128], P(None, 'day', None, 'block')
The draws below stay inside these ranges and needn't reach their ends.
Inputs may be any that keep to these rules, and one draw needn't show every extreme that they name: `valid`: window 0 of every day is usable for every block.
All inputs are finite; a program needn't handle non-finite values.
Results may differ from the reference program's by a relative error of at most 0.015.
Values may be sent and summed in bfloat16 or wider, within the bound.
A program may use at most 256 MiB of HBM per device.

```python
import math
import jax
import jax.numpy as jnp
from jax import lax

F = 128
CB = 128
WIN_DAY = 192
ROUNDS = 2
BLOCKS = 16
DAYS = 8
CHAN = 2048
WINDOWS = 1536


def draw_spectra(key, part):
    key = jax.random.fold_in(key, 11)
    key_base, key_freq, key_window = jax.random.split(key, 3)
    shape = (2, F, WINDOWS, CHAN)
    base = jax.random.normal(key_base, shape, jnp.float32)
    freq_scale = jnp.exp(math.log(10.0) * jax.random.uniform(key_freq, (1, F, 1, CHAN), jnp.float32))
    window_scale = jnp.exp(math.log(10.0) * jax.random.uniform(key_window, (1, 1, WINDOWS, CHAN), jnp.float32))
    values = jnp.clip(base * freq_scale * window_scale, -2000.0, 2000.0)
    return values.astype(jnp.bfloat16)


def draw_valid(key, part):
    key = jax.random.fold_in(key, 23)
    key_level, key_roll = jax.random.split(key, 2)
    levels = jax.random.randint(key_level, (DAYS, BLOCKS), 0, 16)
    day_index = jnp.arange(WINDOWS, dtype=jnp.int32) // WIN_DAY
    first_window = jnp.arange(WINDOWS, dtype=jnp.int32) % WIN_DAY == 0
    threshold = 250 + 700 * (day_index[:, None] * 16 + levels[day_index, :]) // (DAYS * 16)
    rolls = jax.random.randint(key_roll, (WINDOWS, BLOCKS), 0, 1000)
    usable = jnp.logical_or(rolls < threshold, first_window[:, None])
    return usable.astype(jnp.int32)


def setup_inputs(seed: int = 0) -> dict:
    splits = jax.random.split(jax.random.key(seed), 3)
    spectra = draw_spectra(jax.random.fold_in(splits[2], 71), 0)
    valid = draw_valid(jax.random.fold_in(splits[2], 71), 0)
    return {"spectra": spectra, "valid": valid}


EPSILON = 1e-06

def whiten(spectra, valid_cells):
    values = spectra.astype(jnp.float32)
    power = lax.optimization_barrier(jnp.mean(values[0] * values[0] + values[1] * values[1], axis=0))
    scaled = values / jnp.sqrt(power + EPSILON)
    return (scaled * valid_cells.astype(jnp.float32)).astype(jnp.bfloat16)

def cross_terms(first, second):
    left = jnp.concatenate((first[0], first[1]), axis=-1).astype(jnp.float32)
    right = jnp.concatenate((second[0], second[1]), axis=-1).astype(jnp.float32)
    grams = jnp.einsum('fdwc,fdwe->dfce', left, right)
    width = first.shape[-1]
    real_part = grams[:, :, :width, :width] + grams[:, :, width:, width:]
    imag_part = grams[:, :, :width, width:] - grams[:, :, width:, :width]
    return jnp.stack((real_part, imag_part), axis=2)

def round_days(partials):
    rounded = lax.optimization_barrier(partials.astype(jnp.bfloat16))
    return lax.optimization_barrier(jnp.sum(rounded.astype(jnp.float32), axis=0))

def reference(spectra, valid):
    whitened = whiten(spectra, jnp.repeat(valid, CB, axis=1))
    marks = valid.astype(jnp.float32)
    days_view = whitened.reshape((2, F, DAYS, WIN_DAY, CHAN))
    outputs = []
    for round_index in range(ROUNDS):
        shift_key = BLOCKS >> round_index + 1

        def one_block(block_index):
            partner_index = jnp.bitwise_xor(block_index, jnp.int32(shift_key)).astype(jnp.int32)
            first = lax.dynamic_slice_in_dim(days_view, (block_index * CB).astype(jnp.int32), CB, 4)
            second = lax.dynamic_slice_in_dim(days_view, (partner_index * CB).astype(jnp.int32), CB, 4)
            summed = round_days(cross_terms(first, second))
            own_marks = lax.dynamic_index_in_dim(marks, block_index, 1, keepdims=False)
            other_marks = lax.dynamic_index_in_dim(marks, partner_index, 1, keepdims=False)
            shared = jnp.sum(own_marks * other_marks)
            return summed / jnp.sqrt(shared)
        per_block = lax.map(one_block, jnp.arange(BLOCKS, dtype=jnp.int32))
        outputs.append(jnp.transpose(per_block, (1, 2, 0, 3, 4)).reshape((F, 2, CHAN, CB)))
    return jnp.stack(outputs)
```

```python
import functools

import jax
import jax.numpy as jnp
from jax import lax
from jax.experimental import pallas as pl
from jax.experimental.pallas import tpu as pltpu
from jax.sharding import PartitionSpec as P

EPSILON = 1e-06
RING = 4
MESH = pl.DeviceIdType.MESH


def kernel(
    sizes, spectra, marks, out,
    own, taken, scale, scales_in, partial, partials_in, back, back_in, result, counts, counts_in, inverse,
    own_sem, row_send, row_recv, scale_send, scale_recv, count_send, count_recv,
    part_send, part_recv, back_send, back_recv, out_sem,
):
    days, steps, windows, width = sizes
    f32, bf16 = jnp.float32, jnp.bfloat16
    block, day = lax.axis_index("block"), lax.axis_index("day")
    rest_total = lax.axis_size("block") // RING
    row, rest = block // rest_total, block % rest_total
    row_q = row + 1 - 2 * (row % 2)
    row_r = RING - 1 - row
    peers = (row_q * rest_total + rest, row_r * rest_total + rest)
    mine = ((row + 1) // 2) % 2
    other = 1 - mine

    def owner(offset):
        return (day + offset) % days

    def row_copy(side, step):
        half = other if side == 0 else mine
        return pltpu.make_async_remote_copy(
            src_ref=spectra.at[:, :, half, step],
            dst_ref=taken.at[side, step],
            send_sem=row_send.at[side, step],
            recv_sem=row_recv.at[side, step],
            device_id={"block": peers[side]},
            device_id_type=MESH,
        )

    def scale_copy(side):
        return pltpu.make_async_remote_copy(
            src_ref=scale,
            dst_ref=scales_in.at[side],
            send_sem=scale_send.at[side],
            recv_sem=scale_recv.at[side],
            device_id={"block": peers[side]},
            device_id_type=MESH,
        )

    def count_copy(offset):
        return pltpu.make_async_remote_copy(
            src_ref=counts,
            dst_ref=counts_in.at[offset],
            send_sem=count_send.at[offset],
            recv_sem=count_recv.at[offset],
            device_id={"day": owner(offset)},
            device_id_type=MESH,
        )

    def part_copy(step, offset):
        return pltpu.make_async_remote_copy(
            src_ref=partial.at[step, offset],
            dst_ref=partials_in.at[step, offset],
            send_sem=part_send.at[step, offset],
            recv_sem=part_recv.at[step, offset],
            device_id={"day": owner(offset)},
            device_id_type=MESH,
        )

    def back_copy(side, step):
        part = pl.ds(0, 4) if side == 0 else pl.ds(4, 2)
        return pltpu.make_async_remote_copy(
            src_ref=back.at[step, part],
            dst_ref=back_in.at[step, part],
            send_sem=back_send.at[side, step],
            recv_sem=back_recv.at[side, step],
            device_id={"block": peers[side]},
            device_id_type=MESH,
        )

    def own_copy(index):
        return pltpu.make_async_copy(spectra.at[:, index], own.at[:, index], own_sem.at[index])

    def out_copy(kind, step):
        if kind == 0:
            return pltpu.make_async_copy(result.at[1, mine, step], out.at[1, mine, step], out_sem.at[0, step])
        if kind == 1:
            return pltpu.make_async_copy(result.at[0, mine, step], out.at[0, mine, step], out_sem.at[1, step])
        return pltpu.make_async_copy(result.at[:, other, step], out.at[:, other, step], out_sem.at[2, step])

    for index in range(days):
        own_copy(index).start()

    barrier = pltpu.get_barrier_semaphore()
    for side in range(2):
        pl.semaphore_signal(barrier, inc=1, device_id={"block": peers[side]}, device_id_type=MESH)
    for offset in range(1, days):
        pl.semaphore_signal(barrier, inc=1, device_id={"day": owner(offset)}, device_id_type=MESH)
    pl.semaphore_wait(barrier, days + 1)

    for side in range(2):
        row_copy(side, 0).start()

    tile = 48 if windows % 48 == 0 else 16
    scale[...] = jnp.zeros_like(scale)

    @pl.loop(0, days)
    def _(index):
        own_copy(index).wait()

        @pl.loop(0, windows // tile)
        def _(piece):
            rows = pl.ds(pl.multiple_of(piece * tile, tile), tile)
            total = scale[rows, :]
            for half in range(2):
                for step in range(steps):
                    for k in range(2):
                        value = own[k, index, half, step, rows, :].astype(f32)
                        total = total + value * value
            scale[rows, :] = total

    bins = days * 2 * steps
    scale[...] = lax.rsqrt(scale[...] * (1.0 / bins) + EPSILON) * marks[...]
    for side in range(2):
        scale_copy(side).start()

    def whiten(value, factor):
        return (value.astype(f32) * factor).astype(bf16)

    def cross(step):
        @pl.loop(1, days + 1)
        def _(turn):
            offset = turn % days
            index = owner(offset)
            parts = []
            for k in range(2):
                parts.append((
                    whiten(taken[0, step, k, index], scales_in[0]),
                    whiten(taken[1, step, k, index], scales_in[1]),
                    whiten(own[k, index, mine, step], scale[...]),
                ))
            (q_re, r_re, s_re), (q_im, r_im, s_im) = parts
            top = jnp.concatenate((r_re, r_im, s_re, s_im), axis=1)
            low = jnp.concatenate((r_im, -r_re, s_im, -s_re), axis=1)
            dims = (((0,), (0,)), ((), ()))
            gram = lax.dot_general(q_re, top, dims, preferred_element_type=f32)
            gram = gram + lax.dot_general(q_im, low, dims, preferred_element_type=f32)
            for part in range(4):
                partial[step, offset, part] = gram[:, part * width:(part + 1) * width].astype(bf16)

            @pl.when(offset != 0)
            def _():
                part_copy(step, offset).start()

    def reduce(step):
        @pl.loop(1, days)
        def _(offset):
            part_copy(step, offset).wait_recv()

        def total(part):
            value = partial[step, 0, part].astype(f32)
            for offset in range(1, days):
                value = value + partials_in[step, offset, part].astype(f32)
            return value * inverse[pl.ds(part // 2, 1), :]

        re0, im0, re1, im1 = total(0), total(1), total(2), total(3)
        back[step, 0] = re0.astype(bf16)
        back[step, 1] = im0.astype(bf16)
        back[step, 2] = re1.astype(bf16)
        back[step, 3] = im1.astype(bf16)
        back_copy(0, step).start()
        back[step, 4] = re0.T.astype(bf16)
        back[step, 5] = (-im0.T).astype(bf16)
        back_copy(1, step).start()
        result[1, mine, step, 0] = re1.T
        result[1, mine, step, 1] = -im1.T
        out_copy(0, step).start()

    def finish(step):
        back_copy(1, step).wait_recv()
        result[0, mine, step] = back_in[step, pl.ds(4, 2)].astype(f32)
        out_copy(1, step).start()
        back_copy(0, step).wait_recv()
        result[0, other, step] = back_in[step, pl.ds(0, 2)].astype(f32)
        result[1, other, step] = back_in[step, pl.ds(2, 2)].astype(f32)
        out_copy(2, step).start()

    @pl.loop(0, steps + 2)
    def _(turn):
        @pl.when(turn < steps)
        def _():
            @pl.when(turn >= 1)
            def _():
                for side in range(2):
                    row_copy(side, turn - 1).wait_send()

            @pl.when(turn + 1 < steps)
            def _():
                for side in range(2):
                    row_copy(side, turn + 1).start()

            @pl.when(turn == 0)
            def _():
                for side in range(2):
                    scale_copy(side).wait_recv()
                seen_q = jnp.where(scales_in[0] > 0, 1.0, 0.0)
                seen_r = jnp.where(scales_in[1] > 0, 1.0, 0.0)
                first = jnp.sum(seen_q * seen_r, axis=0, keepdims=True)
                second = jnp.sum(seen_q * marks[...], axis=0, keepdims=True)
                counts[...] = jnp.concatenate((first, second) * 4, axis=0)

                @pl.loop(1, days)
                def _(offset):
                    count_copy(offset).start()

            for side in range(2):
                row_copy(side, turn).wait_recv()
            cross(turn)

        @pl.when(turn == 1)
        def _():
            value = counts[...]
            for offset in range(1, days):
                count_copy(offset).wait_recv()
                value = value + counts_in[offset]
            inverse[...] = lax.rsqrt(value)

        @pl.when(jnp.logical_and(turn >= 1, turn < steps + 1))
        def _():
            reduce(turn - 1)

        @pl.when(turn >= 2)
        def _():
            finish(turn - 2)

    for side in range(2):
        row_copy(side, steps - 1).wait_send()
        scale_copy(side).wait_send()

    @pl.loop(1, days)
    def _(offset):
        count_copy(offset).wait_send()

    @pl.loop(0, steps)
    def _(step):
        @pl.loop(1, days)
        def _(offset):
            part_copy(step, offset).wait_send()

        for side in range(2):
            back_copy(side, step).wait_send()
        for kind in range(3):
            out_copy(kind, step).wait()


def per_device(spectra, valid):
    days = lax.axis_size("day")
    _, bins, windows, width = spectra.shape
    steps = bins // days // 2
    f32, bf16 = jnp.float32, jnp.bfloat16
    marks = jnp.broadcast_to(valid.astype(f32), (windows, width))
    dma = pltpu.SemaphoreType.DMA
    stacked = pl.pallas_call(
        functools.partial(kernel, (days, steps, windows, width)),
        out_shape=jax.ShapeDtypeStruct((2, 2, steps, 2, width, width), f32),
        in_specs=[pl.BlockSpec(memory_space=pl.ANY), pl.BlockSpec(memory_space=pltpu.VMEM)],
        out_specs=pl.BlockSpec(memory_space=pl.ANY),
        scratch_shapes=[
            pltpu.VMEM((2, days, 2, steps, windows, width), bf16),
            pltpu.VMEM((2, steps, 2, days, windows, width), bf16),
            pltpu.VMEM((windows, width), f32),
            pltpu.VMEM((2, windows, width), f32),
            pltpu.VMEM((steps, days, 4, width, width), bf16),
            pltpu.VMEM((steps, days, 4, width, width), bf16),
            pltpu.VMEM((steps, 6, width, width), bf16),
            pltpu.VMEM((steps, 6, width, width), bf16),
            pltpu.VMEM((2, 2, steps, 2, width, width), f32),
            pltpu.VMEM((8, width), f32),
            pltpu.VMEM((days, 8, width), f32),
            pltpu.VMEM((8, width), f32),
            dma((days,)),
            dma((2, steps)),
            dma((2, steps)),
            dma((2,)),
            dma((2,)),
            dma((days,)),
            dma((days,)),
            dma((steps, days)),
            dma((steps, days)),
            dma((2, steps)),
            dma((2, steps)),
            dma((3, steps)),
        ],
        compiler_params=pltpu.CompilerParams(
            collective_id=0, has_side_effects=True, vmem_limit_bytes=60 * 1024 * 1024
        ),
        cost_estimate=pl.CostEstimate(flops=6_500_000_000, bytes_accessed=40_000_000, transcendentals=0),
    )(spectra.reshape(2, days, 2, steps, windows, width), marks)
    return stacked.reshape(2, 2 * steps, 2, width, width)


def solution(mesh):
    return jax.shard_map(
        per_device,
        mesh=mesh,
        in_specs=(P(None, None, "day", "block"), P("day", "block")),
        out_specs=P(None, "day", None, "block", None),
        check_vma=False,
    )
```

```python
import functools

import jax
import jax.numpy as jnp
from jax import lax
from jax.experimental import pallas as pl
from jax.experimental.pallas import tpu as pltpu
from jax.sharding import PartitionSpec as P

EPSILON = 1e-06
RING = 4
AHEAD = 16
LATE = 3
VMEM_BYTES = 48 * 1024 * 1024
MESH = pl.DeviceIdType.MESH


def kernel(
    sizes, spectra, valid, out,
    own, taken, scale, scales_in, partial, partials_in, back, counts, counts_in, inverse,
    own_sem, row_send, row_recv, scale_send, scale_recv, count_send, count_recv,
    part_send, part_recv, back_send, back_recv,
):
    days, steps, windows, width = sizes
    units, early = days * steps, max(steps - LATE, 0)
    f32, bf16 = jnp.float32, jnp.bfloat16
    block, day = lax.axis_index("block"), lax.axis_index("day")
    rest_total = lax.axis_size("block") // RING
    row, rest = block // rest_total, block % rest_total
    row_q = row + 1 - 2 * (row % 2)
    row_r = RING - 1 - row
    peers = (row_q * rest_total + rest, row_r * rest_total + rest)
    mine = ((row + 1) // 2) % 2
    other = 1 - mine

    def owner(offset):
        return (day + offset) % days

    def row_copy(side, unit):
        half = other if side == 0 else mine
        step, index = unit // days, owner(unit + 1)
        return pltpu.make_async_remote_copy(
            src_ref=spectra.at[:, index, half, step],
            dst_ref=taken.at[side, step, :, index],
            send_sem=row_send.at[side, unit % AHEAD],
            recv_sem=row_recv.at[side, unit],
            device_id={"block": peers[side]},
            device_id_type=MESH,
        )

    def scale_copy(side):
        return pltpu.make_async_remote_copy(
            src_ref=scale,
            dst_ref=scales_in.at[side],
            send_sem=scale_send.at[side],
            recv_sem=scale_recv.at[side],
            device_id={"block": peers[side]},
            device_id_type=MESH,
        )

    def count_copy(offset):
        return pltpu.make_async_remote_copy(
            src_ref=counts,
            dst_ref=counts_in.at[offset],
            send_sem=count_send.at[offset],
            recv_sem=count_recv.at[offset],
            device_id={"day": owner(offset)},
            device_id_type=MESH,
        )

    def part_copy(step, offset):
        return pltpu.make_async_remote_copy(
            src_ref=partial.at[step, offset],
            dst_ref=partials_in.at[step, offset],
            send_sem=part_send.at[step, offset],
            recv_sem=part_recv.at[step, offset],
            device_id={"day": owner(offset)},
            device_id_type=MESH,
        )

    def back_copy(side, step):
        return pltpu.make_async_remote_copy(
            src_ref=back.at[step, pl.ds(0, 2)] if side == 0 else back.at[step, 2],
            dst_ref=out.at[:, mine, step] if side == 0 else out.at[0, mine, step],
            send_sem=back_send.at[side, step],
            recv_sem=back_recv.at[side, step],
            device_id={"block": peers[side]},
            device_id_type=MESH,
        )

    def back_wait(side, step):
        landed = out.at[:, other, step] if side == 0 else out.at[0, mine, step]
        pltpu.make_async_copy(landed, landed, back_recv.at[side, step]).wait()

    def own_copy(index):
        return pltpu.make_async_copy(spectra.at[:, index], own.at[:, index], own_sem.at[index])

    for index in range(days):
        own_copy(index).start()

    barrier = pltpu.get_barrier_semaphore()
    for side in range(2):
        pl.semaphore_signal(barrier, inc=1, device_id={"block": peers[side]}, device_id_type=MESH)
    for offset in range(1, days):
        pl.semaphore_signal(barrier, inc=1, device_id={"day": owner(offset)}, device_id_type=MESH)
    pl.semaphore_wait(barrier, days + 1)

    @pl.loop(0, AHEAD // 2)
    def _(unit):
        for side in range(2):
            row_copy(side, unit).start()

    tile = 48 if windows % 48 == 0 else 16
    scale[...] = jnp.zeros_like(scale)

    @pl.loop(0, days)
    def _(index):
        own_copy(index).wait()

        @pl.loop(0, windows // tile)
        def _(piece):
            rows = pl.ds(pl.multiple_of(piece * tile, tile), tile)
            total = scale[rows, :]
            for half in range(2):
                for step in range(steps):
                    for k in range(2):
                        value = own[k, index, half, step, rows, :].astype(f32)
                        total = total + value * value
            scale[rows, :] = total

    bins = days * 2 * steps
    marks = jnp.broadcast_to(valid[...].astype(f32), (width, windows)).T
    scale[...] = lax.rsqrt(scale[...] * (1.0 / bins) + EPSILON) * marks
    for side in range(2):
        scale_copy(side).start()

    @pl.loop(AHEAD // 2, AHEAD)
    def _(unit):
        for side in range(2):
            row_copy(side, unit).start()

    def whiten(value, factor):
        return (value.astype(f32) * factor).astype(bf16)

    def cross(step):
        @pl.loop(1, days + 1)
        def _(turn):
            offset = turn % days
            index = owner(offset)
            unit = step * days + turn - 1
            for side in range(2):
                row_copy(side, unit).wait_recv()
            parts = []
            for k in range(2):
                parts.append((
                    whiten(taken[0, step, k, index], scales_in[0]),
                    whiten(taken[1, step, k, index], scales_in[1]),
                    whiten(own[k, index, mine, step], scale[...]),
                ))
            (q_re, r_re, s_re), (q_im, r_im, s_im) = parts
            top = jnp.concatenate((r_re, r_im, s_re, s_im), axis=1)
            low = jnp.concatenate((r_im, -r_re, s_im, -s_re), axis=1)
            dims = (((0,), (0,)), ((), ()))
            gram = lax.dot_general(q_re, top, dims, preferred_element_type=f32)
            gram = gram + lax.dot_general(q_im, low, dims, preferred_element_type=f32)
            for part in range(4):
                partial[step, offset, part] = gram[:, part * width:(part + 1) * width].astype(bf16)

            @pl.when(offset != 0)
            def _():
                part_copy(step, offset).start()

            @pl.when(unit + AHEAD < units)
            def _():
                for side in range(2):
                    row_copy(side, unit).wait_send()
                    row_copy(side, unit + AHEAD).start()

    def reduce(step):
        @pl.loop(1, days)
        def _(offset):
            part_copy(step, offset).wait_recv()

        def total(part):
            value = partial[step, 0, part].astype(f32)
            for offset in range(1, days):
                value = value + partials_in[step, offset, part].astype(f32)
            return value * inverse[pl.ds(part // 2, 1), :]

        re0, im0, re1, im1 = total(0), total(1), total(2), total(3)
        back[step, 0, 0] = re0.astype(bf16)
        back[step, 0, 1] = im0.astype(bf16)
        back[step, 1, 0] = re1.astype(bf16)
        back[step, 1, 1] = im1.astype(bf16)
        back[step, 2, 0] = re0.T.astype(bf16)
        back[step, 2, 1] = (-im0.T).astype(bf16)

        @pl.when(jnp.logical_or(step < early, step == steps - 1))
        def _():
            for side in range(2):
                back_copy(side, step).start()

        out[1, mine, step, 0] = re1.T.astype(bf16)
        out[1, mine, step, 1] = (-im1.T).astype(bf16)

    for side in range(2):
        scale_copy(side).wait_recv()
    seen_q = jnp.where(scales_in[0] > 0, 1.0, 0.0)
    seen_r = jnp.where(scales_in[1] > 0, 1.0, 0.0)
    seen = jnp.where(scale[...] > 0, 1.0, 0.0)
    first = jnp.sum(seen_q * seen_r, axis=0, keepdims=True)
    second = jnp.sum(seen_q * seen, axis=0, keepdims=True)
    counts[...] = jnp.concatenate((first, second) * 4, axis=0)

    @pl.loop(1, days)
    def _(offset):
        count_copy(offset).start()

    @pl.loop(0, steps + 1)
    def _(turn):
        @pl.when(turn < steps)
        def _():
            cross(turn)

        @pl.when(turn == 1)
        def _():
            value = counts[...]
            for offset in range(1, days):
                count_copy(offset).wait_recv()
                value = value + counts_in[offset]
            inverse[...] = lax.rsqrt(value)

        @pl.when(turn == steps)
        def _():
            @pl.loop(early, steps - 1)
            def _(step):
                for side in range(2):
                    back_copy(side, step).start()

        @pl.when(turn >= 1)
        def _():
            reduce(turn - 1)

    @pl.loop(units - AHEAD, units)
    def _(unit):
        for side in range(2):
            row_copy(side, unit).wait_send()

    for side in range(2):
        scale_copy(side).wait_send()

    @pl.loop(1, days)
    def _(offset):
        count_copy(offset).wait_send()

    @pl.loop(0, steps)
    def _(step):
        @pl.loop(1, days)
        def _(offset):
            part_copy(step, offset).wait_send()

        for side in range(2):
            back_copy(side, step).wait_send()
            back_wait(side, step)


def per_device(spectra, valid):
    days = lax.axis_size("day")
    _, bins, windows, width = spectra.shape
    steps = bins // days // 2
    f32, bf16 = jnp.float32, jnp.bfloat16
    dma = pltpu.SemaphoreType.DMA
    stacked = pl.pallas_call(
        functools.partial(kernel, (days, steps, windows, width)),
        out_shape=pltpu.VMEM((2, 2, steps, 2, width, width), bf16),
        in_specs=[pl.BlockSpec(memory_space=pl.ANY), pl.BlockSpec(memory_space=pltpu.VMEM)],
        out_specs=pl.BlockSpec(memory_space=pltpu.VMEM),
        scratch_shapes=[
            pltpu.VMEM((2, days, 2, steps, windows, width), bf16),
            pltpu.VMEM((2, steps, 2, days, windows, width), bf16),
            pltpu.VMEM((windows, width), f32),
            pltpu.VMEM((2, windows, width), f32),
            pltpu.VMEM((steps, days, 4, width, width), bf16),
            pltpu.VMEM((steps, days, 4, width, width), bf16),
            pltpu.VMEM((steps, 3, 2, width, width), bf16),
            pltpu.VMEM((8, width), f32),
            pltpu.VMEM((days, 8, width), f32),
            pltpu.VMEM((8, width), f32),
            dma((days,)),
            dma((2, AHEAD)),
            dma((2, days * steps)),
            dma((2,)),
            dma((2,)),
            dma((days,)),
            dma((days,)),
            dma((steps, days)),
            dma((steps, days)),
            dma((2, steps)),
            dma((2, steps)),
        ],
        compiler_params=pltpu.CompilerParams(
            collective_id=0, has_side_effects=True, vmem_limit_bytes=VMEM_BYTES
        ),
        cost_estimate=pl.CostEstimate(flops=6_500_000_000, bytes_accessed=40_000_000, transcendentals=0),
    )(spectra.reshape(2, days, 2, steps, windows, width), valid.reshape(1, windows))
    return stacked.reshape(2, 2 * steps, 2, width, width).astype(f32)


def solution(mesh):
    return jax.shard_map(
        per_device,
        mesh=mesh,
        in_specs=(P(None, None, "day", "block"), P("day", "block")),
        out_specs=P(None, "day", None, "block", None),
        check_vma=False,
    )
```

```python
import functools

import jax
import jax.numpy as jnp
from jax import lax
from jax.experimental import pallas as pl
from jax.experimental.pallas import tpu as pltpu
from jax.sharding import PartitionSpec as P

EPSILON = 1e-06
RING = 4
LATE = 3
VMEM_BYTES = 48 * 1024 * 1024
MESH = pl.DeviceIdType.MESH


def kernel(
    sizes, spectra, valid, out,
    own, taken, scale, scale_out, scales_in, partial, partials_in, back, counts, counts_in, inverse,
    seen_row, arrived, valid_sem, own_sem, row_send, row_recv, scale_send, scale_recv, count_send, count_recv,
    part_send, part_recv, back_send, back_recv,
):
    days, steps, windows, width = sizes
    last, early = steps - 1, steps - LATE
    f32, bf16 = jnp.float32, jnp.bfloat16
    block, day = lax.axis_index("block"), lax.axis_index("day")
    rest_total = lax.axis_size("block") // RING
    row, rest = block // rest_total, block % rest_total
    row_q = row + 1 - 2 * (row % 2)
    row_r = RING - 1 - row
    peers = (row_q * rest_total + rest, row_r * rest_total + rest)
    mine = ((row + 1) // 2) % 2
    other = 1 - mine

    along, across = day % RING, day // RING
    nearest = [across * RING + (along + 1) % RING, across * RING + (along + RING - 1) % RING]
    if days > RING:
        nearest.append((1 - across) * RING + along)

    def owner(offset):
        return (day + offset) % days

    def row_copy(side, step, index=None):
        half = other if side == 0 else mine
        slot = step if index is None else last + index
        index = slice(None) if index is None else index
        return pltpu.make_async_remote_copy(
            src_ref=spectra.at[:, index, half, step],
            dst_ref=taken.at[side, step, :, index],
            send_sem=row_send.at[side, slot],
            recv_sem=row_recv.at[side, slot],
            device_id={"block": peers[side]},
            device_id_type=MESH,
        )

    def scale_copy(side):
        return pltpu.make_async_remote_copy(
            src_ref=scale_out,
            dst_ref=scales_in.at[side],
            send_sem=scale_send.at[side],
            recv_sem=scale_recv.at[side],
            device_id={"block": peers[side]},
            device_id_type=MESH,
        )

    def count_copy(offset):
        return pltpu.make_async_remote_copy(
            src_ref=counts,
            dst_ref=counts_in.at[offset],
            send_sem=count_send.at[offset],
            recv_sem=count_recv.at[offset],
            device_id={"day": owner(offset)},
            device_id_type=MESH,
        )

    def part_copy(step, offset):
        return pltpu.make_async_remote_copy(
            src_ref=partial.at[step, offset],
            dst_ref=partials_in.at[step, offset],
            send_sem=part_send.at[step, offset],
            recv_sem=part_recv.at[step, offset],
            device_id={"day": owner(offset)},
            device_id_type=MESH,
        )

    def back_copy(side, step):
        return pltpu.make_async_remote_copy(
            src_ref=back.at[step, pl.ds(0, 2)] if side == 0 else back.at[step, 2],
            dst_ref=out.at[:, mine, step] if side == 0 else out.at[0, mine, step],
            send_sem=back_send.at[side, step],
            recv_sem=back_recv.at[side, step],
            device_id={"block": peers[side]},
            device_id_type=MESH,
        )

    def back_wait(side, step):
        landed = out.at[:, other, step] if side == 0 else out.at[0, mine, step]
        pltpu.make_async_copy(landed, landed, back_recv.at[side, step]).wait()

    def own_copy(index):
        return pltpu.make_async_copy(spectra.at[:, index], own.at[:, index], own_sem.at[index])

    valid_copy = pltpu.make_async_copy(valid, seen_row, valid_sem)
    valid_copy.start()
    for index in range(days):
        own_copy(index).start()

    barrier = pltpu.get_barrier_semaphore()
    for side in range(2):
        pl.semaphore_signal(barrier, inc=1, device_id={"block": peers[side]}, device_id_type=MESH)
    for near in nearest:
        pl.semaphore_signal(barrier, inc=1, device_id={"day": near}, device_id_type=MESH)
    pl.semaphore_wait(barrier, 2 + len(nearest))

    for side in range(2):
        row_copy(side, 0).start()

    for hop in range(2):
        for near in nearest:
            pl.semaphore_signal(arrived.at[hop], inc=1, device_id={"day": near}, device_id_type=MESH)
        pl.semaphore_wait(arrived.at[hop], len(nearest))

    tile = 48 if windows % 48 == 0 else 16
    scale[...] = jnp.zeros_like(scale)

    @pl.loop(0, days)
    def _(index):
        own_copy(index).wait()

        @pl.loop(0, windows // tile)
        def _(piece):
            rows = pl.ds(pl.multiple_of(piece * tile, tile), tile)
            total = scale[rows, :]
            for half in range(2):
                for step in range(steps):
                    for k in range(2):
                        value = own[k, index, half, step, rows, :].astype(f32)
                        total = total + value * value
            scale[rows, :] = total

    bins = days * 2 * steps
    valid_copy.wait()
    marks = jnp.broadcast_to(seen_row[...].astype(f32), (width, windows)).T
    scale[...] = lax.rsqrt(scale[...] * (1.0 / bins) + EPSILON) * marks
    scale_out[...] = scale[...].astype(bf16)
    for side in range(2):
        scale_copy(side).start()

    for side in range(2):
        row_copy(side, 1).start()

    def whiten(value, factor):
        return (value.astype(f32) * factor).astype(bf16)

    def cross(step):
        @pl.when(step < last)
        def _():
            for side in range(2):
                row_copy(side, step).wait_recv()
                row_copy(side, step).wait_send()

                @pl.when(step + 2 < last)
                def _():
                    row_copy(side, step + 2).start()

        @pl.when(step + 2 == last)
        def _():
            @pl.loop(1, days + 1)
            def _(turn):
                for side in range(2):
                    row_copy(side, last, owner(turn)).start()

        @pl.loop(1, days + 1)
        def _(turn):
            offset = turn % days
            index = owner(offset)

            @pl.when(step == last)
            def _():
                for side in range(2):
                    row_copy(side, last, index).wait_recv()

            parts = []
            for k in range(2):
                parts.append((
                    whiten(taken[0, step, k, index], scales_in[0].astype(f32)),
                    whiten(taken[1, step, k, index], scales_in[1].astype(f32)),
                    whiten(own[k, index, mine, step], scale[...]),
                ))
            (q_re, r_re, s_re), (q_im, r_im, s_im) = parts
            top = jnp.concatenate((r_re, r_im, s_re, s_im), axis=1)
            low = jnp.concatenate((r_im, -r_re, s_im, -s_re), axis=1)
            dims = (((0,), (0,)), ((), ()))
            gram = lax.dot_general(q_re, top, dims, preferred_element_type=f32)
            gram = gram + lax.dot_general(q_im, low, dims, preferred_element_type=f32)
            for part in range(4):
                partial[step, offset, part] = gram[:, part * width:(part + 1) * width].astype(bf16)

            @pl.when(offset != 0)
            def _():
                part_copy(step, offset).start()

    def reduce(step):
        @pl.loop(1, days)
        def _(offset):
            part_copy(step, offset).wait_recv()

        def total(part):
            value = partial[step, 0, part].astype(f32)
            for offset in range(1, days):
                value = value + partials_in[step, offset, part].astype(f32)
            return value * inverse[pl.ds(part // 2, 1), :]

        re0, im0, re1, im1 = total(0), total(1), total(2), total(3)
        back[step, 0, 0] = re0.astype(bf16)
        back[step, 0, 1] = im0.astype(bf16)
        back[step, 1, 0] = re1.astype(bf16)
        back[step, 1, 1] = im1.astype(bf16)
        back[step, 2, 0] = re0.T.astype(bf16)
        back[step, 2, 1] = (-im0.T).astype(bf16)

        @pl.when(jnp.logical_or(step < early, step == steps - 1))
        def _():
            for side in range(2):
                back_copy(side, step).start()

        out[1, mine, step, 0] = re1.T.astype(bf16)
        out[1, mine, step, 1] = (-im1.T).astype(bf16)

    for side in range(2):
        scale_copy(side).wait_recv()
    seen_q = jnp.where(scales_in[0] > 0, 1.0, 0.0)
    seen_r = jnp.where(scales_in[1] > 0, 1.0, 0.0)
    seen = jnp.where(scale[...] > 0, 1.0, 0.0)
    first = jnp.sum(seen_q * seen_r, axis=0, keepdims=True)
    second = jnp.sum(seen_q * seen, axis=0, keepdims=True)
    counts[...] = jnp.concatenate((first, second) * 4, axis=0)

    @pl.loop(1, days)
    def _(offset):
        count_copy(offset).start()

    @pl.loop(0, steps + 1)
    def _(turn):
        @pl.when(turn < steps)
        def _():
            cross(turn)

        @pl.when(turn == 1)
        def _():
            value = counts[...]
            for offset in range(1, days):
                count_copy(offset).wait_recv()
                value = value + counts_in[offset]
            inverse[...] = lax.rsqrt(value)

        @pl.when(turn == steps)
        def _():
            @pl.loop(early, steps - 1)
            def _(step):
                for side in range(2):
                    back_copy(side, step).start()

        @pl.when(turn >= 1)
        def _():
            reduce(turn - 1)

    @pl.loop(0, days)
    def _(index):
        for side in range(2):
            row_copy(side, last, index).wait_send()

    for side in range(2):
        scale_copy(side).wait_send()

    @pl.loop(1, days)
    def _(offset):
        count_copy(offset).wait_send()

    @pl.loop(0, steps)
    def _(step):
        @pl.loop(1, days)
        def _(offset):
            part_copy(step, offset).wait_send()

    @pl.loop(0, steps)
    def _(step):
        for side in range(2):
            back_copy(side, step).wait_send()
            back_wait(side, step)


def per_device(spectra, valid):
    days = lax.axis_size("day")
    _, bins, windows, width = spectra.shape
    steps = bins // days // 2
    f32, bf16 = jnp.float32, jnp.bfloat16
    dma = pltpu.SemaphoreType.DMA
    stacked = pl.pallas_call(
        functools.partial(kernel, (days, steps, windows, width)),
        out_shape=pltpu.VMEM((2, 2, steps, 2, width, width), bf16),
        in_specs=[pl.BlockSpec(memory_space=pltpu.HBM)] * 2,
        out_specs=pl.BlockSpec(memory_space=pltpu.VMEM),
        scratch_shapes=[
            pltpu.VMEM((2, days, 2, steps, windows, width), bf16),
            pltpu.VMEM((2, steps, 2, days, windows, width), bf16),
            pltpu.VMEM((windows, width), f32),
            pltpu.VMEM((windows, width), bf16),
            pltpu.VMEM((2, windows, width), bf16),
            pltpu.VMEM((steps, days, 4, width, width), bf16),
            pltpu.VMEM((steps, days, 4, width, width), bf16),
            pltpu.VMEM((steps, 3, 2, width, width), bf16),
            pltpu.VMEM((8, width), f32),
            pltpu.VMEM((days, 8, width), f32),
            pltpu.VMEM((8, width), f32),
            pltpu.VMEM((1, windows), jnp.int32),
            pltpu.SemaphoreType.REGULAR((2,)),
            dma,
            dma((days,)),
            dma((2, steps - 1 + days)),
            dma((2, steps - 1 + days)),
            dma((2,)),
            dma((2,)),
            dma((days,)),
            dma((days,)),
            dma((steps, days)),
            dma((steps, days)),
            dma((2, steps)),
            dma((2, steps)),
        ],
        compiler_params=pltpu.CompilerParams(
            collective_id=0, has_side_effects=True, vmem_limit_bytes=VMEM_BYTES
        ),
        cost_estimate=pl.CostEstimate(flops=6_500_000_000, bytes_accessed=40_000_000, transcendentals=0),
    )(spectra.reshape(2, days, 2, steps, windows, width), pltpu.with_memory_space_constraint(valid.reshape(1, windows), pltpu.HBM))
    return stacked.reshape(2, 2 * steps, 2, width, width).astype(f32)


def solution(mesh):
    return jax.shard_map(
        per_device,
        mesh=mesh,
        in_specs=(P(None, None, "day", "block"), P("day", "block")),
        out_specs=P(None, "day", None, "block", None),
        check_vma=False,
    )
```

```python
import functools

import jax
import jax.numpy as jnp
from jax import lax
from jax.experimental import pallas as pl
from jax.experimental.pallas import tpu as pltpu
from jax.sharding import PartitionSpec as P

EPSILON = 1e-06
RING = 4
LATE = 2
PIECES = 8
VMEM_BYTES = 48 * 1024 * 1024
MESH = pl.DeviceIdType.MESH


def kernel(
    sizes, spectra, valid, out,
    own, taken, scale, scale_out, scales_in, partial, partials_in, back, counts, counts_in, inverse,
    seen_row, arrived, valid_sem, own_sem, row_send, row_recv, scale_send, scale_recv, count_send, count_recv,
    part_send, part_recv, back_send, back_recv,
):
    days, steps, windows, width = sizes
    last, early = steps - 1, steps - LATE
    f32, bf16 = jnp.float32, jnp.bfloat16
    block, day = lax.axis_index("block"), lax.axis_index("day")
    rest_total = lax.axis_size("block") // RING
    row, rest = block // rest_total, block % rest_total
    row_q = row + 1 - 2 * (row % 2)
    row_r = RING - 1 - row
    peers = (row_q * rest_total + rest, row_r * rest_total + rest)
    mine = ((row + 1) // 2) % 2
    other = 1 - mine

    along, across = day % RING, day // RING
    place = along + across * (days - 1 - 2 * along)

    def ringed(spot):
        spot = spot % days
        far = spot // RING
        return far * RING + spot % RING + far * (RING - 1 - 2 * (spot % RING))

    after, before = ringed(place + 1), ringed(place + days - 1)

    def owner(offset):
        return (day + offset) % days

    def row_copy(side, step, index=None, source=own):
        half = other if side == 0 else mine
        slot = step if index is None else last + index
        index = slice(None) if index is None else index
        return pltpu.make_async_remote_copy(
            src_ref=source.at[:, index, half, step],
            dst_ref=taken.at[side, step, :, index],
            send_sem=row_send.at[side, slot],
            recv_sem=row_recv.at[side, slot],
            device_id={"block": peers[side]},
            device_id_type=MESH,
        )

    def scale_copy(side):
        return pltpu.make_async_remote_copy(
            src_ref=scale_out,
            dst_ref=scales_in.at[side],
            send_sem=scale_send.at[side],
            recv_sem=scale_recv.at[side],
            device_id={"block": peers[side]},
            device_id_type=MESH,
        )

    def count_copy(offset):
        return pltpu.make_async_remote_copy(
            src_ref=counts,
            dst_ref=counts_in.at[offset],
            send_sem=count_send.at[offset],
            recv_sem=count_recv.at[offset],
            device_id={"day": owner(offset)},
            device_id_type=MESH,
        )

    def part_copy(step, offset):
        return pltpu.make_async_remote_copy(
            src_ref=partial.at[step, offset],
            dst_ref=partials_in.at[step, offset],
            send_sem=part_send.at[step, offset],
            recv_sem=part_recv.at[step, offset],
            device_id={"day": owner(offset)},
            device_id_type=MESH,
        )

    def back_copy(side, step):
        return pltpu.make_async_remote_copy(
            src_ref=back.at[step, pl.ds(0, 2)] if side == 0 else back.at[step, 2],
            dst_ref=out.at[:, mine, step] if side == 0 else out.at[0, mine, step],
            send_sem=back_send.at[side, step],
            recv_sem=back_recv.at[side, step],
            device_id={"block": peers[side]},
            device_id_type=MESH,
        )

    def back_wait(side, step):
        landed = out.at[:, other, step] if side == 0 else out.at[0, mine, step]
        pltpu.make_async_copy(landed, landed, back_recv.at[side, step]).wait()

    def own_copy(index):
        return pltpu.make_async_copy(spectra.at[:, index], own.at[:, index], own_sem.at[index])

    valid_copy = pltpu.make_async_copy(valid, seen_row, valid_sem)
    valid_copy.start()
    for index in range(days):
        own_copy(index).start()

    barrier = pltpu.get_barrier_semaphore()
    for side in range(2):
        pl.semaphore_signal(barrier, inc=1, device_id={"block": peers[side]}, device_id_type=MESH)
    pl.semaphore_signal(barrier, inc=1, device_id={"day": before}, device_id_type=MESH)
    pl.semaphore_wait(barrier, 3)

    for side in range(2):
        row_copy(side, 0, source=spectra).start()

    pl.semaphore_signal(arrived.at[0], inc=1, device_id={"day": after}, device_id_type=MESH)
    pl.semaphore_wait(arrived.at[0], 1)
    for hop in range(1, days // 2):
        for near in (after, before):
            pl.semaphore_signal(arrived.at[hop], inc=1, device_id={"day": near}, device_id_type=MESH)
        pl.semaphore_wait(arrived.at[hop], 2)

    tile = 48 if windows % 48 == 0 else 16
    scale[...] = jnp.zeros_like(scale)

    @pl.loop(0, days)
    def _(index):
        own_copy(index).wait()

        @pl.loop(0, windows // tile)
        def _(piece):
            rows = pl.ds(pl.multiple_of(piece * tile, tile), tile)
            total = scale[rows, :]
            for half in range(2):
                for step in range(steps):
                    for k in range(2):
                        value = own[k, index, half, step, rows, :].astype(f32)
                        total = total + value * value
            scale[rows, :] = total

    bins = days * 2 * steps
    valid_copy.wait()
    marks = jnp.broadcast_to(seen_row[...].astype(f32), (width, windows)).T
    scale[...] = lax.rsqrt(scale[...] * (1.0 / bins) + EPSILON) * marks
    scale_out[...] = scale[...].astype(bf16)
    for side in range(2):
        scale_copy(side).start()

    def whiten(value, factor):
        return (value.astype(f32) * factor).astype(bf16)

    def prepare(step):
        factor = scale[...]

        @pl.loop(0, days)
        def _(index):
            for half in range(2):
                for k in range(2):
                    own[k, index, half, step] = whiten(own[k, index, half, step], factor)

    prepare(1)
    for side in range(2):
        row_copy(side, 1).start()
    prepare(0)

    def cross(step):
        @pl.when(step + 2 <= last)
        def _():
            prepare(step + 2)

        @pl.when(step < last)
        def _():
            for side in range(2):
                row_copy(side, step).wait_recv()
                row_copy(side, step).wait_send()

                @pl.when(step + 2 < last)
                def _():
                    row_copy(side, step + 2).start()

        @pl.when(step + 2 == last)
        def _():
            @pl.loop(1, days + 1)
            def _(turn):
                for side in range(2):
                    row_copy(side, last, owner(turn)).start()

        @pl.loop(1, days + 1)
        def _(turn):
            offset = turn % days
            index = owner(offset)

            @pl.when(step == last)
            def _():
                for side in range(2):
                    row_copy(side, last, index).wait_recv()

            @pl.when(step == 0)
            def _():
                for side in range(2):
                    factor = scales_in[side].astype(f32)
                    for k in range(2):
                        taken[side, 0, k, index] = whiten(taken[side, 0, k, index], factor)

            q_re, q_im = taken[0, step, 0, index], taken[0, step, 1, index]
            r_re, r_im = taken[1, step, 0, index], taken[1, step, 1, index]
            s_re, s_im = own[0, index, mine, step], own[1, index, mine, step]
            top = jnp.concatenate((r_re, r_im, s_re, s_im), axis=1)
            low = jnp.concatenate((r_im, -r_re, s_im, -s_re), axis=1)
            dims = (((0,), (0,)), ((), ()))
            gram = lax.dot_general(q_re, top, dims, preferred_element_type=f32)
            gram = gram + lax.dot_general(q_im, low, dims, preferred_element_type=f32)
            for part in range(4):
                partial[step, offset, part] = gram[:, part * width:(part + 1) * width].astype(bf16)

            @pl.when(offset != 0)
            def _():
                part_copy(step, offset).start()

    def reduce(step):
        @pl.loop(1, days)
        def _(offset):
            part_copy(step, offset).wait_recv()

        def total(part):
            value = partial[step, 0, part].astype(f32)
            for offset in range(1, days):
                value = value + partials_in[step, offset, part].astype(f32)
            return value * inverse[pl.ds(part // 2, 1), :]

        re0, im0, re1, im1 = total(0), total(1), total(2), total(3)
        back[step, 0, 0] = re0.astype(bf16)
        back[step, 0, 1] = im0.astype(bf16)
        back[step, 1, 0] = re1.astype(bf16)
        back[step, 1, 1] = im1.astype(bf16)
        back[step, 2, 0] = re0.T.astype(bf16)
        back[step, 2, 1] = (-im0.T).astype(bf16)

        @pl.when(jnp.logical_or(step < early, step == steps - 1))
        def _():
            for side in range(2):
                back_copy(side, step).start()

        out[1, mine, step, 0] = re1.T.astype(bf16)
        out[1, mine, step, 1] = (-im1.T).astype(bf16)

    for side in range(2):
        scale_copy(side).wait_recv()
    seen_q = jnp.where(scales_in[0] > 0, 1.0, 0.0)
    seen_r = jnp.where(scales_in[1] > 0, 1.0, 0.0)
    seen = jnp.where(scale[...] > 0, 1.0, 0.0)
    first = jnp.sum(seen_q * seen_r, axis=0, keepdims=True)
    second = jnp.sum(seen_q * seen, axis=0, keepdims=True)
    counts[...] = jnp.concatenate((first, second) * 4, axis=0)

    @pl.loop(1, days)
    def _(offset):
        count_copy(offset).start()

    @pl.loop(0, steps + 1)
    def _(turn):
        @pl.when(turn < steps)
        def _():
            cross(turn)

        @pl.when(turn == 1)
        def _():
            value = counts[...]
            for offset in range(1, days):
                count_copy(offset).wait_recv()
                value = value + counts_in[offset]
            inverse[...] = lax.rsqrt(value)

        @pl.when(turn == steps)
        def _():
            @pl.loop(early, steps - 1)
            def _(step):
                for side in range(2):
                    back_copy(side, step).start()

        @pl.when(turn >= 1)
        def _():
            reduce(turn - 1)

    @pl.loop(0, days)
    def _(index):
        for side in range(2):
            row_copy(side, last, index).wait_send()

    for side in range(2):
        scale_copy(side).wait_send()

    @pl.loop(1, days)
    def _(offset):
        count_copy(offset).wait_send()

    @pl.loop(0, steps)
    def _(step):
        @pl.loop(1, days)
        def _(offset):
            part_copy(step, offset).wait_send()

    @pl.loop(0, steps)
    def _(step):
        for side in range(2):
            back_copy(side, step).wait_send()
            back_wait(side, step)


def widen(narrow, wide, staged, sem):
    pieces = narrow.shape[0]

    def piece_copy(piece):
        return pltpu.make_async_copy(staged.at[piece], wide.at[piece], sem.at[piece])

    for piece in range(pieces):
        staged[piece] = narrow[piece].astype(jnp.float32)
        piece_copy(piece).start()
    for piece in range(pieces):
        piece_copy(piece).wait()


def per_device(spectra, valid):
    days = lax.axis_size("day")
    _, bins, windows, width = spectra.shape
    steps = bins // days // 2
    f32, bf16 = jnp.float32, jnp.bfloat16
    dma = pltpu.SemaphoreType.DMA
    stacked = pl.pallas_call(
        functools.partial(kernel, (days, steps, windows, width)),
        out_shape=pltpu.VMEM((2, 2, steps, 2, width, width), bf16),
        in_specs=[pl.BlockSpec(memory_space=pltpu.HBM)] * 2,
        out_specs=pl.BlockSpec(memory_space=pltpu.VMEM),
        scratch_shapes=[
            pltpu.VMEM((2, days, 2, steps, windows, width), bf16),
            pltpu.VMEM((2, steps, 2, days, windows, width), bf16),
            pltpu.VMEM((windows, width), f32),
            pltpu.VMEM((windows, width), bf16),
            pltpu.VMEM((2, windows, width), bf16),
            pltpu.VMEM((steps, days, 4, width, width), bf16),
            pltpu.VMEM((steps, days, 4, width, width), bf16),
            pltpu.VMEM((steps, 3, 2, width, width), bf16),
            pltpu.VMEM((8, width), f32),
            pltpu.VMEM((days, 8, width), f32),
            pltpu.VMEM((8, width), f32),
            pltpu.VMEM((1, windows), jnp.int32),
            pltpu.SemaphoreType.REGULAR((days // 2,)),
            dma,
            dma((days,)),
            dma((2, steps - 1 + days)),
            dma((2, steps - 1 + days)),
            dma((2,)),
            dma((2,)),
            dma((days,)),
            dma((days,)),
            dma((steps, days)),
            dma((steps, days)),
            dma((2, steps)),
            dma((2, steps)),
        ],
        compiler_params=pltpu.CompilerParams(
            collective_id=0, has_side_effects=True, vmem_limit_bytes=VMEM_BYTES
        ),
        cost_estimate=pl.CostEstimate(flops=6_500_000_000, bytes_accessed=40_000_000, transcendentals=0),
    )(spectra.reshape(2, days, 2, steps, windows, width), pltpu.with_memory_space_constraint(valid.reshape(1, windows), pltpu.HBM))
    pieces = (PIECES, 8 * steps * width // PIECES, width)
    stacked = pl.pallas_call(
        widen,
        out_shape=jax.ShapeDtypeStruct(pieces, f32),
        in_specs=[pl.BlockSpec(memory_space=pltpu.VMEM)],
        out_specs=pl.BlockSpec(memory_space=pl.ANY),
        scratch_shapes=[pltpu.VMEM(pieces, f32), dma((PIECES,))],
        compiler_params=pltpu.CompilerParams(vmem_limit_bytes=16 * 1024 * 1024),
    )(stacked.reshape(pieces))
    return stacked.reshape(2, 2 * steps, 2, width, width)


def solution(mesh):
    return jax.shard_map(
        per_device,
        mesh=mesh,
        in_specs=(P(None, None, "day", "block"), P("day", "block")),
        out_specs=P(None, "day", None, "block", None),
        check_vma=False,
    )
```

```python
import functools

import jax
import jax.numpy as jnp
from jax import lax
from jax.experimental import pallas as pl
from jax.experimental.pallas import tpu as pltpu
from jax.sharding import PartitionSpec as P

EPSILON = 1e-06
RING = 4
LATE = 2
GAP = 1
PIECES = 8
VMEM_BYTES = 48 * 1024 * 1024
MESH = pl.DeviceIdType.MESH


def kernel(
    sizes, spectra, valid, result,
    out, own, taken, scale, scale_out, scales_in, partial, partials_in, back, counts, counts_in, inverse,
    seen_row, arrived, valid_sem, own_sem, row_send, row_recv, scale_send, scale_recv, count_send, count_recv,
    part_send, part_recv, back_send, back_recv,
):
    days, steps, windows, width = sizes
    last, early = steps - 1, steps - LATE
    f32, bf16 = jnp.float32, jnp.bfloat16
    block, day = lax.axis_index("block"), lax.axis_index("day")
    rest_total = lax.axis_size("block") // RING
    row, rest = block // rest_total, block % rest_total
    row_q = row + 1 - 2 * (row % 2)
    row_r = RING - 1 - row
    peers = (row_q * rest_total + rest, row_r * rest_total + rest)
    mine = ((row + 1) // 2) % 2
    other = 1 - mine

    along, across = day % RING, day // RING
    place = along + across * (days - 1 - 2 * along)

    def ringed(spot):
        spot = spot % days
        far = spot // RING
        return far * RING + spot % RING + far * (RING - 1 - 2 * (spot % RING))

    after, before = ringed(place + 1), ringed(place + days - 1)

    def owner(offset):
        return (day + offset) % days

    def row_copy(side, step, index=None, source=own):
        half = other if side == 0 else mine
        slot = step if index is None else last + index
        index = slice(None) if index is None else index
        return pltpu.make_async_remote_copy(
            src_ref=source.at[:, index, half, step],
            dst_ref=taken.at[side, step, :, index],
            send_sem=row_send.at[side, slot],
            recv_sem=row_recv.at[side, slot],
            device_id={"block": peers[side]},
            device_id_type=MESH,
        )

    def scale_copy(side):
        return pltpu.make_async_remote_copy(
            src_ref=scale_out,
            dst_ref=scales_in.at[side],
            send_sem=scale_send.at[side],
            recv_sem=scale_recv.at[side],
            device_id={"block": peers[side]},
            device_id_type=MESH,
        )

    def count_copy(offset):
        return pltpu.make_async_remote_copy(
            src_ref=counts,
            dst_ref=counts_in.at[offset],
            send_sem=count_send.at[offset],
            recv_sem=count_recv.at[offset],
            device_id={"day": owner(offset)},
            device_id_type=MESH,
        )

    def part_copy(step, offset):
        return pltpu.make_async_remote_copy(
            src_ref=partial.at[step, offset],
            dst_ref=partials_in.at[step, offset],
            send_sem=part_send.at[step, offset],
            recv_sem=part_recv.at[step, offset],
            device_id={"day": owner(offset)},
            device_id_type=MESH,
        )

    def back_copy(side, step):
        return pltpu.make_async_remote_copy(
            src_ref=back.at[step, pl.ds(0, 2)] if side == 0 else back.at[step, 2],
            dst_ref=out.at[:, mine, step] if side == 0 else out.at[0, mine, step],
            send_sem=back_send.at[side, step],
            recv_sem=back_recv.at[side, step],
            device_id={"block": peers[side]},
            device_id_type=MESH,
        )

    def back_wait(side, step):
        landed = out.at[:, other, step] if side == 0 else out.at[0, mine, step]
        pltpu.make_async_copy(landed, landed, back_recv.at[side, step]).wait()

    def own_copy(index):
        return pltpu.make_async_copy(spectra.at[:, index], own.at[:, index], own_sem.at[index])

    valid_copy = pltpu.make_async_copy(valid, seen_row, valid_sem)
    valid_copy.start()
    for index in range(days):
        own_copy(index).start()

    barrier = pltpu.get_barrier_semaphore()
    for side in range(2):
        pl.semaphore_signal(barrier, inc=1, device_id={"block": peers[side]}, device_id_type=MESH)
    pl.semaphore_signal(barrier, inc=1, device_id={"day": before}, device_id_type=MESH)
    pl.semaphore_wait(barrier, 3)

    for side in range(2):
        row_copy(side, 0, source=spectra).start()

    pl.semaphore_signal(arrived.at[0], inc=1, device_id={"day": after}, device_id_type=MESH)
    pl.semaphore_wait(arrived.at[0], 1)
    for hop in range(1, days // 2):
        for near in (after, before):
            pl.semaphore_signal(arrived.at[hop], inc=1, device_id={"day": near}, device_id_type=MESH)
        pl.semaphore_wait(arrived.at[hop], 2)

    tile = 48 if windows % 48 == 0 else 16
    scale[...] = jnp.zeros_like(scale)

    @pl.loop(0, days)
    def _(index):
        own_copy(index).wait()

        @pl.loop(0, windows // tile)
        def _(piece):
            rows = pl.ds(pl.multiple_of(piece * tile, tile), tile)
            total = scale[rows, :]
            for half in range(2):
                for step in range(steps):
                    for k in range(2):
                        value = own[k, index, half, step, rows, :].astype(f32)
                        total = total + value * value
            scale[rows, :] = total

    bins = days * 2 * steps
    valid_copy.wait()
    marks = jnp.broadcast_to(seen_row[...].astype(f32), (width, windows)).T
    scale[...] = lax.rsqrt(scale[...] * (1.0 / bins) + EPSILON) * marks
    scale_out[...] = scale[...].astype(bf16)
    for side in range(2):
        scale_copy(side).start()

    def whiten(value, factor):
        return (value.astype(f32) * factor).astype(bf16)

    def prepare(step):
        factor = scale[...]

        @pl.loop(0, days)
        def _(index):
            for half in range(2):
                for k in range(2):
                    own[k, index, half, step] = whiten(own[k, index, half, step], factor)

    prepare(1)
    for side in range(2):
        row_copy(side, 1).start()
    prepare(0)

    def reduce(step):
        @pl.loop(1, days)
        def _(offset):
            part_copy(step, offset).wait_recv()

        def total(part):
            value = partial[step, 0, part].astype(f32)
            for offset in range(1, days):
                value = value + partials_in[step, offset, part].astype(f32)
            return value * inverse[pl.ds(part // 2, 1), :]

        re0, im0, re1, im1 = total(0), total(1), total(2), total(3)
        back[step, 0, 0] = re0.astype(bf16)
        back[step, 0, 1] = im0.astype(bf16)
        back[step, 1, 0] = re1.astype(bf16)
        back[step, 1, 1] = im1.astype(bf16)
        back[step, 2, 0] = re0.T.astype(bf16)
        back[step, 2, 1] = (-im0.T).astype(bf16)

        @pl.when(jnp.logical_or(step < early, step == steps - 1))
        def _():
            for side in range(2):
                back_copy(side, step).start()

        out[1, mine, step, 0] = re1.T.astype(bf16)
        out[1, mine, step, 1] = (-im1.T).astype(bf16)

    def cross(step):
        @pl.when(step + 2 <= last)
        def _():
            prepare(step + 2)

        @pl.when(step < last)
        def _():
            for side in range(2):
                row_copy(side, step).wait_recv()
                row_copy(side, step).wait_send()

                @pl.when(step + 2 < last)
                def _():
                    row_copy(side, step + 2).start()

        @pl.when(step + 2 == last)
        def _():
            @pl.loop(1, days + 1)
            def _(turn):
                for side in range(2):
                    row_copy(side, last, owner(turn)).start()

        @pl.loop(1, days + 1)
        def _(turn):
            offset = turn % days
            index = owner(offset)

            @pl.when(step == last)
            def _():
                for side in range(2):
                    row_copy(side, last, index).wait_recv()

            @pl.when(step == 0)
            def _():
                for side in range(2):
                    factor = scales_in[side].astype(f32)
                    for k in range(2):
                        taken[side, 0, k, index] = whiten(taken[side, 0, k, index], factor)

            q_re, q_im = taken[0, step, 0, index], taken[0, step, 1, index]
            r_re, r_im = taken[1, step, 0, index], taken[1, step, 1, index]
            s_re, s_im = own[0, index, mine, step], own[1, index, mine, step]
            top = jnp.concatenate((r_re, r_im, s_re, s_im), axis=1)
            low = jnp.concatenate((r_im, -r_re, s_im, -s_re), axis=1)
            dims = (((0,), (0,)), ((), ()))
            gram = lax.dot_general(q_re, top, dims, preferred_element_type=f32)
            gram = gram + lax.dot_general(q_im, low, dims, preferred_element_type=f32)
            for part in range(4):
                partial[step, offset, part] = gram[:, part * width:(part + 1) * width].astype(bf16)

            @pl.when(offset != 0)
            def _():
                part_copy(step, offset).start()

            @pl.when(jnp.logical_and(turn == days - GAP, step == last))
            def _():
                reduce(step - 1)

    for side in range(2):
        scale_copy(side).wait_recv()
    seen_q = jnp.where(scales_in[0] > 0, 1.0, 0.0)
    seen_r = jnp.where(scales_in[1] > 0, 1.0, 0.0)
    seen = jnp.where(scale[...] > 0, 1.0, 0.0)
    first = jnp.sum(seen_q * seen_r, axis=0, keepdims=True)
    second = jnp.sum(seen_q * seen, axis=0, keepdims=True)
    counts[...] = jnp.concatenate((first, second) * 4, axis=0)

    @pl.loop(1, days)
    def _(offset):
        count_copy(offset).start()

    @pl.loop(0, steps + 1)
    def _(turn):
        @pl.when(turn < steps)
        def _():
            cross(turn)

        @pl.when(turn == 1)
        def _():
            value = counts[...]
            for offset in range(1, days):
                count_copy(offset).wait_recv()
                value = value + counts_in[offset]
            inverse[...] = lax.rsqrt(value)

        @pl.when(turn == steps)
        def _():
            @pl.loop(early, steps - 1)
            def _(step):
                for side in range(2):
                    back_copy(side, step).start()

        @pl.when(jnp.logical_and(turn >= 1, turn != last))
        def _():
            reduce(turn - 1)

    @pl.loop(0, days)
    def _(index):
        for side in range(2):
            row_copy(side, last, index).wait_send()

    for side in range(2):
        scale_copy(side).wait_send()

    @pl.loop(1, days)
    def _(offset):
        count_copy(offset).wait_send()

    @pl.loop(0, steps)
    def _(step):
        @pl.loop(1, days)
        def _(offset):
            part_copy(step, offset).wait_send()

    @pl.loop(0, steps)
    def _(step):
        for side in range(2):
            back_copy(side, step).wait_send()
            back_wait(side, step)
        result[:, :, step] = out[:, :, step].astype(f32)


def store(held, stored, sem):
    def piece_copy(piece):
        return pltpu.make_async_copy(held.at[piece], stored.at[piece], sem.at[piece])

    for piece in range(PIECES):
        piece_copy(piece).start()
    for piece in range(PIECES):
        piece_copy(piece).wait()


def per_device(spectra, valid):
    days = lax.axis_size("day")
    _, bins, windows, width = spectra.shape
    steps = bins // days // 2
    f32, bf16 = jnp.float32, jnp.bfloat16
    dma = pltpu.SemaphoreType.DMA
    stacked = pl.pallas_call(
        functools.partial(kernel, (days, steps, windows, width)),
        out_shape=pltpu.VMEM((2, 2, steps, 2, width, width), f32),
        in_specs=[pl.BlockSpec(memory_space=pltpu.HBM)] * 2,
        out_specs=pl.BlockSpec(memory_space=pltpu.VMEM),
        scratch_shapes=[
            pltpu.VMEM((2, 2, steps, 2, width, width), bf16),
            pltpu.VMEM((2, days, 2, steps, windows, width), bf16),
            pltpu.VMEM((2, steps, 2, days, windows, width), bf16),
            pltpu.VMEM((windows, width), f32),
            pltpu.VMEM((windows, width), bf16),
            pltpu.VMEM((2, windows, width), bf16),
            pltpu.VMEM((steps, days, 4, width, width), bf16),
            pltpu.VMEM((steps, days, 4, width, width), bf16),
            pltpu.VMEM((steps, 3, 2, width, width), bf16),
            pltpu.VMEM((8, width), f32),
            pltpu.VMEM((days, 8, width), f32),
            pltpu.VMEM((8, width), f32),
            pltpu.VMEM((1, windows), jnp.int32),
            pltpu.SemaphoreType.REGULAR((days // 2,)),
            dma,
            dma((days,)),
            dma((2, steps - 1 + days)),
            dma((2, steps - 1 + days)),
            dma((2,)),
            dma((2,)),
            dma((days,)),
            dma((days,)),
            dma((steps, days)),
            dma((steps, days)),
            dma((2, steps)),
            dma((2, steps)),
        ],
        compiler_params=pltpu.CompilerParams(
            collective_id=0, has_side_effects=True, vmem_limit_bytes=VMEM_BYTES
        ),
        cost_estimate=pl.CostEstimate(flops=6_500_000_000, bytes_accessed=40_000_000, transcendentals=0),
    )(spectra.reshape(2, days, 2, steps, windows, width), pltpu.with_memory_space_constraint(valid.reshape(1, windows), pltpu.HBM))
    pieces = (PIECES, 8 * steps * width // PIECES, width)
    stacked = pl.pallas_call(
        store,
        out_shape=jax.ShapeDtypeStruct(pieces, f32),
        in_specs=[pl.BlockSpec(memory_space=pltpu.VMEM)],
        out_specs=pl.BlockSpec(memory_space=pl.ANY),
        scratch_shapes=[dma((PIECES,))],
        compiler_params=pltpu.CompilerParams(vmem_limit_bytes=8 * 1024 * 1024),
    )(stacked.reshape(pieces))
    return stacked.reshape(2, 2 * steps, 2, width, width)


def solution(mesh):
    return jax.shard_map(
        per_device,
        mesh=mesh,
        in_specs=(P(None, None, "day", "block"), P("day", "block")),
        out_specs=P(None, "day", None, "block", None),
        check_vma=False,
    )
```
